128 devices in a mesh: section: 8 (over z, core), seq: 16 (over x, y).
Axes of the slice: x: 4, y: 4, z: 4, core: 2. Of those that a mesh axis runs over, the one named last changes fastest.
Arguments:
- patch_tokens: bfloat16 [4, 256, 3072], P(None, 'seq'), may hold values from -31 to 31
- patch_order: int32 [4], replicated, may hold values from 0 to 3, each once
- modulation: float32 [8, 3, 3072], P('section'), may hold values from -3 to 3
- norm_gain: float32 [8, 2, 128], P('section'), may hold values from 1 to 2
- project_weight: bfloat16 [8, 3072, 3, 16, 128], P('section', None, None, 'seq'), may hold values from -0.109375 to 0.109375
- output_weight: bfloat16 [8, 2048, 3072], P('section'), may hold values from -0.125 to 0.125
- stale_cache: bfloat16 [8, 2, 4, 256, 16, 128], P('section', None, None, None, 'seq'), may hold values from -31 to 31
Outputs:
- block_outputs: bfloat16 [8, 4, 256, 3072], P('section', None, 'seq')
- fresh_cache: bfloat16 [8, 2, 4, 256, 16, 128], P('section', None, None, None, 'seq')
The draws below stay inside these ranges and needn't reach their ends.
Inputs may be any that keep to these rules, and one draw needn't show every extreme that they name: Each of the 4 patches appears once in patch_order.
All inputs are finite; a program needn't handle non-finite values.
Results may differ from the reference program's by a relative error of at most 0.02.
Values may be sent and summed in bfloat16 or wider, within the bound.
A program may use at most 192 MiB of HBM per device.

```python
import math
import jax
import jax.numpy as jnp
from jax import lax

D = 3072
HD = 128
HEADS = 16
PATCHES = 4
LAYERS = 8
PATCH_TOK = 256
TOKENS = 1024


def spread(scale_key, sample):
    row_key, col_key = jax.random.split(scale_key)
    row_scale = jnp.power(10.0, jax.random.uniform(row_key, sample.shape[:-1] + (1,), jnp.float32, -0.5, 0.5))
    col_scale = jnp.power(10.0, jax.random.uniform(col_key, (sample.shape[-1],), jnp.float32, -0.5, 0.5))
    return sample * row_scale * col_scale


def draw_patch_tokens(key, part):
    key = jax.random.fold_in(key, 11)
    shape_all = (PATCHES, PATCH_TOK, D)
    scale_key, base_key = jax.random.split(key, 2)
    sample = jax.random.truncated_normal(base_key, -3.0, 3.0, shape_all, jnp.float32)
    return spread(scale_key, sample).astype(jnp.bfloat16)


def draw_stale_cache(key, part):
    key = jax.random.fold_in(key, 23)
    shape_all = (LAYERS, 2, PATCHES, PATCH_TOK, HEADS, HD)
    scale_key, base_key = jax.random.split(key, 2)
    sample = jax.random.truncated_normal(base_key, -3.0, 3.0, shape_all, jnp.float32)
    return spread(scale_key, sample).astype(jnp.bfloat16)


def block_scale(stream_key, extent, cuts, smallest, top_value):
    loudness, own = 1.0, jax.random.fold_in(stream_key, 6)
    for dim, parts in cuts:
        heights = jnp.exp(jax.random.uniform(jax.random.fold_in(own, dim), (parts,), jnp.float32, smallest / len(cuts), top_value / len(cuts)))
        loudness = loudness * jnp.repeat(heights, extent[dim] // parts).reshape([-1 if axis == dim else 1 for axis in range(len(extent))])
    return loudness


def normal_values(own_key, shape, width, bound, cuts=(), dtype=jnp.bfloat16):
    level = block_scale(own_key, shape, cuts, -0.22, 0.18) if cuts else 1.0
    array = jax.random.normal(own_key, shape, jnp.float32) * width * level
    return jnp.minimum(jnp.maximum(array, -bound), bound).astype(dtype)


def setup_inputs(seed: int = 0) -> dict:
    key_of = jax.random.split(jax.random.key(seed), 8)
    patch_tokens = draw_patch_tokens(jax.random.fold_in(key_of[7], 71), 0)
    patch_order = jax.random.permutation(key_of[1], PATCHES).astype(jnp.int32)
    modulation = normal_values(key_of[2], (LAYERS, 3, D), 1.0, 3.0, ((0, 8),), jnp.float32)
    norm_gain = jnp.clip(jnp.exp(math.log(2.0) - 0.6931472 * jax.random.uniform(key_of[3], (LAYERS, 2, HD), jnp.float32) ** block_scale(key_of[3], (LAYERS, 2, HD), ((0, 8),), -0.2, 0.2)), 1.0, 2.0)
    project_weight = normal_values(key_of[4], (LAYERS, D, 3, HEADS, HD), D ** -0.5, 0.109375, ((0, 8), (3, 16)))
    output_weight = normal_values(key_of[5], (LAYERS, HEADS * HD, D), (HEADS * HD) ** -0.5, 0.125, ((0, 8),))
    stale_cache = draw_stale_cache(jax.random.fold_in(key_of[7], 71), 0)
    return {"patch_tokens": patch_tokens, "patch_order": patch_order, "modulation": modulation, "norm_gain": norm_gain, "project_weight": project_weight, "output_weight": output_weight, "stale_cache": stale_cache}


def modulated_norm(block_input, modulation_rows):
    values = block_input.astype(jnp.float32)
    centre = lax.optimization_barrier(jnp.mean(values, axis=-1, keepdims=True))
    spread_sq = lax.optimization_barrier(jnp.mean((values - centre) * (values - centre), axis=-1, keepdims=True))
    normed = (values - centre) * lax.rsqrt(spread_sq + 1e-06)
    return (normed * (1.0 + modulation_rows[1]) + modulation_rows[0]).astype(jnp.bfloat16)

def unit_rows(values, gain):
    floats = values.astype(jnp.float32)
    return floats * lax.rsqrt(lax.optimization_barrier(jnp.mean(floats * floats, axis=-1, keepdims=True)) + 1e-06) * gain

def block_patch(block_input, modulation_rows, gains, project_layer, output_layer, buffer, patch_index):
    normed = modulated_norm(block_input, modulation_rows)
    projected = jnp.dot(normed, project_layer.reshape(D, 3 * HEADS * HD), preferred_element_type=jnp.float32)
    projected = projected.astype(jnp.bfloat16).reshape(PATCH_TOK, 3, HEADS, HD)
    anchor = jnp.zeros((), jnp.int32)
    fresh_rows = jnp.stack((projected[:, 1], projected[:, 2]))[:, None]
    buffer = lax.dynamic_update_slice(buffer, fresh_rows, (anchor, patch_index.astype(jnp.int32), anchor, anchor, anchor))
    all_keys = buffer[0].reshape(TOKENS, HEADS, HD)
    all_values = buffer[1].reshape(TOKENS, HEADS, HD)
    query_unit = (unit_rows(projected[:, 0], gains[0]) / math.sqrt(HD)).astype(jnp.bfloat16)
    key_unit = unit_rows(all_keys, gains[1]).astype(jnp.bfloat16)
    scores = jnp.einsum('qhd,khd->hqk', query_unit.astype(jnp.float32), key_unit.astype(jnp.float32))
    exp_scores = jnp.exp(scores)
    denominator = lax.optimization_barrier(jnp.sum(exp_scores, axis=-1))
    softmax_weights = exp_scores.astype(jnp.bfloat16)
    summed = jnp.einsum('hqk,khd->qhd', softmax_weights.astype(jnp.float32), all_values.astype(jnp.float32))
    attended = (summed / denominator.T[:, :, None]).astype(jnp.bfloat16)
    branch = jnp.dot(attended.reshape(PATCH_TOK, HEADS * HD), output_layer, preferred_element_type=jnp.float32)
    result = (block_input.astype(jnp.float32) + modulation_rows[2] * branch).astype(jnp.bfloat16)
    return (result, buffer)

def reference(patch_tokens, patch_order, modulation, norm_gain, project_weight, output_weight, stale_cache):
    current = patch_tokens
    outputs_all = []
    buffers_all = []
    for layer_index in range(LAYERS):
        buffer = stale_cache[layer_index]
        results = current
        for position in range(PATCHES):
            patch_index = patch_order[position].astype(jnp.int32)
            block_input = lax.dynamic_index_in_dim(current, patch_index, 0, keepdims=False)
            produced, buffer = block_patch(block_input, modulation[layer_index], norm_gain[layer_index], project_weight[layer_index], output_weight[layer_index], buffer, patch_index)
            results = lax.dynamic_update_index_in_dim(results, produced, patch_index, 0)
        outputs_all.append(results)
        buffers_all.append(buffer)
        current = results
    return (jnp.stack(outputs_all), jnp.stack(buffers_all))
```

```python
import functools
import math

import jax
import jax.numpy as jnp
from jax import lax
from jax.experimental import pallas as pl
from jax.experimental.pallas import tpu as pltpu
from jax.sharding import PartitionSpec as P

MESH = pl.DeviceIdType.MESH
SIDE = 4
GROUP = SIDE * SIDE


def unit_rows(values, gain):
    floats = values.astype(jnp.float32)
    return floats * lax.rsqrt(jnp.mean(floats * floats, axis=-1, keepdims=True) + 1e-06) * gain


def normalized(values, shift, scale):
    centre = jnp.mean(values, axis=-1, keepdims=True)
    moved = values - centre
    spread_sq = jnp.mean(moved * moved, axis=-1, keepdims=True)
    return (moved * lax.rsqrt(spread_sq + 1e-06) * (1.0 + scale) + shift).astype(jnp.bfloat16)


def kernel(
    sections, patches, rows, width, head,
    order_ref, tokens_ref, mod_ref, gain_ref, project_hbm, output_hbm, stale_ref,
    out_ref, cache_ref,
    project_w, output_w, land, residual, next_mod, normed, attended, heads_land,
    key_unit, value_rows, total,
    weight_sem, mod_sem, line_sem, own_sem, residual_sem, relay_sem, head_sem,
    first_sent, feed_sent, residual_sent, relay_sent, head_sent,
):
    section = lax.axis_index("section")
    me = lax.axis_index("seq")
    x, y = me // SIDE, me % SIDE
    half = width // 2
    patch_rows = rows * GROUP
    is_first = section == 0
    has_next = section < sections - 1

    def chip(dx, dy):
        return ((x + dx) % SIDE) * SIDE + (y + dy) % SIDE

    def block(index):
        return pl.ds(pl.multiple_of(index * rows, rows), rows)

    def send(source, target, sent, arrived, device):
        pltpu.make_async_remote_copy(
            src_ref=source, dst_ref=target, send_sem=sent, recv_sem=arrived,
            device_id=device, device_id_type=MESH,
        ).start()

    def wait(ref, sem):
        pltpu.make_async_copy(ref, ref, sem).wait()

    project_copies = [
        pltpu.make_async_copy(
            project_hbm.at[part], project_w.at[:, part * head : (part + 1) * head],
            weight_sem.at[1 + part],
        )
        for part in range(3)
    ]
    for copy in project_copies:
        copy.start()
    output_copy = pltpu.make_async_copy(output_hbm, output_w, weight_sem.at[0])
    output_copy.start()

    barrier = pltpu.get_barrier_semaphore()

    def greet(device):
        pl.semaphore_signal(barrier, inc=1, device_id=device, device_id_type=MESH)

    def greet_lines(other):
        greet((other, me))
        for step in range(1, SIDE):
            greet((other, chip(step, 0)))
            greet((other, chip(0, step)))

    @pl.loop(1, GROUP)
    def _(step):
        greet((section, chip(step // SIDE, step % SIDE)))

    @pl.when(has_next)
    def _():
        greet_lines(section + 1)

    @pl.when(jnp.logical_not(is_first))
    def _():
        greet_lines(section - 1)

    lines = 2 * (SIDE - 1) + 1
    @pl.when(jnp.logical_and(has_next, jnp.logical_not(is_first)))
    def _():
        pl.semaphore_wait(barrier, GROUP - 1 + 2 * lines)

    @pl.when(jnp.logical_or(jnp.logical_not(has_next), is_first))
    def _():
        pl.semaphore_wait(barrier, GROUP - 1 + lines)

    def send_lines(source, patch, other, sent):
        for step in (2, 1, 3):
            send(source, land.at[patch, block(me), :], sent.at[patch],
                 line_sem.at[patch, 0, step - 1], (other, chip(step, 0)))
            send(source, land.at[patch, block(me), :], sent.at[patch],
                 line_sem.at[patch, 1, step - 1], (other, chip(0, step)))

    def feed(patch):
        values = residual[patch].astype(jnp.float32)
        land[patch, block(me), :] = normalized(values, mod_ref[0:1, :], mod_ref[1:2, :])
        send_lines(land.at[patch, block(me), :], patch, section, feed_sent)

    def relay(patch):
        for step in (1, 3, 2):
            source = block(chip(0, -step))
            wait(land.at[patch, source, :], line_sem.at[patch, 1, step - 1])
            for onward in (2, 1, 3):
                part = land.at[patch, source, pl.ds(0, half)]
                send(part, part, relay_sent.at[patch], relay_sem.at[patch],
                     (section, chip(onward, 0)))
            source = block(chip(-step, 0))
            wait(land.at[patch, source, :], line_sem.at[patch, 0, step - 1])
            for onward in (2, 1, 3):
                part = land.at[patch, source, pl.ds(half, half)]
                send(part, part, relay_sent.at[patch], relay_sem.at[patch],
                     (section, chip(0, onward)))

    @pl.when(jnp.logical_not(is_first))
    def _():
        send(mod_ref, next_mod, mod_sem.at[0], mod_sem.at[1], (section - 1, me))

    @pl.when(is_first)
    def _():
        for patch in range(patches):
            residual[patch] = tokens_ref[order_ref[patch]]
        feed(0)

    for patch in range(1, patches):
        place = pl.ds(patch * patch_rows, patch_rows)
        key_unit[place, :] = unit_rows(stale_ref[0, order_ref[patch]], gain_ref[1:2, :]).astype(
            jnp.bfloat16
        )
        value_rows[place, :] = stale_ref[1, order_ref[patch]]

    relay(0)

    @pl.when(is_first)
    def _():
        feed(1)

    for copy in project_copies:
        copy.wait()

    @pl.loop(0, patches)
    def _(patch):
        @pl.when(jnp.logical_not(is_first))
        def _():
            wait(land.at[patch, block(me), :], own_sem.at[patch])

        wait(land.at[patch, pl.ds(0, (SIDE - 1) ** 2 * rows), :], relay_sem.at[patch])
        projected = jnp.dot(
            land[patch], project_w[...], preferred_element_type=jnp.float32
        ).astype(jnp.bfloat16)
        place = pl.ds(pl.multiple_of(patch * patch_rows, patch_rows), patch_rows)
        keys, values = projected[:, head : 2 * head], projected[:, 2 * head :]
        cache_ref[0, place, :] = keys
        cache_ref[1, place, :] = values
        key_unit[place, :] = unit_rows(keys, gain_ref[1:2, :]).astype(jnp.bfloat16)
        value_rows[place, :] = values
        query_unit = (
            unit_rows(projected[:, :head], gain_ref[0:1, :]) / math.sqrt(head)
        ).astype(jnp.bfloat16)
        scores = lax.dot_general(
            query_unit, key_unit[...], (((1,), (1,)), ((), ())),
            preferred_element_type=jnp.float32,
        )
        exp_scores = jnp.exp(scores)
        denominator = jnp.sum(exp_scores, axis=-1, keepdims=True)
        summed = jnp.dot(
            exp_scores.astype(jnp.bfloat16), value_rows[...], preferred_element_type=jnp.float32
        )
        attended[patch] = (summed / denominator).astype(jnp.bfloat16)
        own_columns = pl.ds(pl.multiple_of(me * head, head), head)

        @pl.loop(0, GROUP - 1)
        def _(step):
            dx, dy = (GROUP - 1 - step) // SIDE, (GROUP - 1 - step) % SIDE
            to = chip(dx, dy)
            send(attended.at[patch, block(to), :], heads_land.at[patch, :, own_columns],
                 head_sent.at[patch], head_sem.at[patch, (SIDE - dx) % SIDE], (section, to))

        heads_land[patch, :, own_columns] = attended[patch, block(me), :]

        @pl.when(patch < patches - 1)
        def _():
            relay(patch + 1)

        @pl.when(jnp.logical_and(is_first, patch < patches - 2))
        def _():
            feed(patch + 2)

        @pl.when(patch == 0)
        def _():
            output_copy.wait()

        total[...] = jnp.zeros_like(total)

        @pl.loop(0, SIDE)
        def _(step):
            gap = step + step // 2 - 2 * (step // 3)
            columns = pl.ds(
                pl.multiple_of(((x + gap) % SIDE) * (SIDE * head), SIDE * head), SIDE * head
            )

            @pl.when(step == 0)
            def _():
                wait(heads_land.at[patch, :, pl.ds(0, (SIDE - 1) * head)],
                     head_sem.at[patch, 0])

            @pl.when(step > 0)
            def _():
                wait(heads_land.at[patch, :, pl.ds(0, SIDE * head)], head_sem.at[patch, gap])

            for first in range(0, width, half):
                total[:, first : first + half] += jnp.dot(
                    heads_land[patch, :, columns], output_w[columns, first : first + half],
                    preferred_element_type=jnp.float32,
                )

        @pl.when(jnp.logical_not(is_first))
        def _():
            wait(residual.at[patch], residual_sem.at[patch])

        produced = (
            residual[patch].astype(jnp.float32) + mod_ref[2:3, :] * total[...]
        ).astype(jnp.bfloat16)
        out_ref[patch] = produced

        @pl.when(has_next)
        def _():
            @pl.when(patch == 0)
            def _():
                wait(next_mod, mod_sem.at[1])

            normed[patch] = normalized(
                out_ref[patch].astype(jnp.float32), next_mod[0:1, :], next_mod[1:2, :]
            )
            send_lines(normed.at[patch], patch, section + 1, first_sent)
            send(normed.at[patch], land.at[patch, block(me), :], first_sent.at[patch],
                 own_sem.at[patch], (section + 1, me))
            send(out_ref.at[patch], residual.at[patch], residual_sent.at[patch],
                 residual_sem.at[patch], (section + 1, me))

    @pl.when(jnp.logical_not(is_first))
    def _():
        wait(next_mod, mod_sem.at[0])

    @pl.loop(0, patches)
    def _(patch):
        wait(heads_land.at[patch, :, pl.ds(0, (GROUP - 1) * head)], head_sent.at[patch])
        wait(land.at[patch, pl.ds(0, (SIDE - 1) ** 2 * rows), :], relay_sent.at[patch])

        @pl.when(is_first)
        def _():
            wait(land.at[patch, pl.ds(0, (lines - 1) * rows), :], feed_sent.at[patch])

        @pl.when(has_next)
        def _():
            wait(land.at[patch, pl.ds(0, lines * rows), :], first_sent.at[patch])
            wait(residual.at[patch], residual_sent.at[patch])


def body(
    patch_tokens, patch_order, modulation, norm_gain, project_weight, output_weight, stale_cache
):
    sections = lax.axis_size("section")
    patches, rows, width = patch_tokens.shape
    head = project_weight.shape[-1]
    patch_rows = rows * GROUP
    tokens = patches * patch_rows
    columns = project_weight.reshape(width, 3, head).transpose(1, 0, 2)
    vmem, hbm = pl.BlockSpec(memory_space=pltpu.VMEM), pl.BlockSpec(memory_space=pl.ANY)
    bf16, f32, dma = jnp.bfloat16, jnp.float32, pltpu.SemaphoreType.DMA
    results, cache = pl.pallas_call(
        functools.partial(kernel, sections, patches, rows, width, head),
        out_shape=(
            jax.ShapeDtypeStruct((patches, rows, width), bf16),
            jax.ShapeDtypeStruct((2, tokens, head), bf16),
        ),
        in_specs=[pl.BlockSpec(memory_space=pltpu.SMEM), vmem, vmem, vmem, hbm, hbm, vmem],
        out_specs=(vmem, vmem),
        scratch_shapes=[
            pltpu.VMEM((width, 3 * head), bf16),
            pltpu.VMEM((GROUP * head, width), bf16),
            pltpu.VMEM((patches, patch_rows, width), bf16),
            pltpu.VMEM((patches, rows, width), bf16),
            pltpu.VMEM((3, width), f32),
            pltpu.VMEM((patches, rows, width), bf16),
            pltpu.VMEM((patches, patch_rows, head), bf16),
            pltpu.VMEM((patches, rows, GROUP * head), bf16),
            pltpu.VMEM((tokens, head), bf16),
            pltpu.VMEM((tokens, head), bf16),
            pltpu.VMEM((rows, width), f32),
            dma((4,)), dma((2,)), dma((patches, 2, SIDE - 1)), dma((patches,)), dma((patches,)),
            dma((patches,)), dma((patches, SIDE)),
            dma((patches,)), dma((patches,)), dma((patches,)), dma((patches,)), dma((patches,)),
        ],
        compiler_params=pltpu.CompilerParams(
            collective_id=0, has_side_effects=True, vmem_limit_bytes=48 << 20
        ),
        name="blocks",
    )(
        patch_order, patch_tokens, modulation[0], norm_gain[0], columns, output_weight[0],
        stale_cache[0].reshape(2, patches, patch_rows, head),
    )
    steps = jnp.arange(patches, dtype=jnp.int32)
    place = jnp.sum(
        jnp.where(patch_order[None, :] == steps[:, None], steps[None, :], 0), axis=1
    )
    cache = cache.reshape(2, patches, patch_rows, 1, head)
    results = jnp.stack([lax.dynamic_index_in_dim(results, place[p], 0, False) for p in range(patches)])
    cache = jnp.stack(
        [lax.dynamic_index_in_dim(cache, place[p], 1, False) for p in range(patches)], axis=1
    )
    return (results[None], cache[None])


def solution(mesh):
    in_specs = (
        P(None, "seq", None),
        P(),
        P("section", None, None),
        P("section", None, None),
        P("section", None, None, "seq", None),
        P("section", None, None),
        P("section", None, None, None, "seq", None),
    )
    out_specs = (P("section", None, "seq", None), P("section", None, None, None, "seq", None))
    return jax.shard_map(body, mesh=mesh, in_specs=in_specs, out_specs=out_specs, check_vma=False)
```

```python
import functools
import math

import jax
import jax.numpy as jnp
from jax import lax
from jax.experimental import pallas as pl
from jax.experimental.pallas import tpu as pltpu
from jax.sharding import PartitionSpec as P

MESH = pl.DeviceIdType.MESH
SIDE = 4
GROUP = SIDE * SIDE
HELD = 4

BLOCK_ORDER = [
    spot
    for colour in range(SIDE)
    for spot in (SIDE * colour, SIDE * ((colour + 2) % SIDE) + 1)
] + [
    SIDE * ((1 if colour < 2 else 0) + 2 * turn) + 2 + colour % 2
    for colour in range(SIDE)
    for turn in range(2)
]


def unit_rows(values, gain):
    floats = values.astype(jnp.float32)
    return floats * lax.rsqrt(jnp.mean(floats * floats, axis=-1, keepdims=True) + 1e-06) * gain


def normalized(values, shift, scale):
    centre = jnp.mean(values, axis=-1, keepdims=True)
    moved = values - centre
    spread_sq = jnp.mean(moved * moved, axis=-1, keepdims=True)
    return (moved * lax.rsqrt(spread_sq + 1e-06) * (1.0 + scale) + shift).astype(jnp.bfloat16)


def kernel(
    sections, patches, rows, width, head,
    tokens_hbm, order_hbm, mod_hbm, gain_hbm, project_hbm, output_hbm, stale_hbm,
    out_ref, cache_ref,
    order, tokens, mod, gain, stale, project_w, output_w, first, incoming, produced, land,
    attended, heads_land, key_unit, value_rows, total, results, fresh,
    next_mod, normed, mod_sem, normed_sent,
    load_sem, token_sent, incoming_sem, produced_sent, land_sem, land_sent, head_sem, head_sent,
):
    section = lax.axis_index("section")
    me = lax.axis_index("seq")
    x, y = me // SIDE, me % SIDE
    patch_rows = rows * GROUP
    is_first = section == 0
    has_next = section < sections - 1
    is_even = section % 2 == 0
    is_odd = section % 2 == 1

    def chip(dx, dy):
        return ((x + dx) % SIDE) * SIDE + (y + dy) % SIDE

    def held_start(chip_x, chip_y, kind):
        if kind == 0:
            return pl.multiple_of(((chip_x + 2 * chip_y) % SIDE) * (2 * rows), 2 * rows)
        return pl.multiple_of(
            patch_rows // 2 + ((2 * chip_x + chip_y) % SIDE) * (2 * rows), 2 * rows
        )

    def block(index):
        return pl.ds(pl.multiple_of(index * rows, rows), rows)

    def send(source, target, sent, arrived, device):
        pltpu.make_async_remote_copy(
            src_ref=source, dst_ref=target, send_sem=sent, recv_sem=arrived,
            device_id=device, device_id_type=MESH,
        ).start()

    def wait(ref, sem):
        pltpu.make_async_copy(ref, ref, sem).wait()

    loads = [
        pltpu.make_async_copy(source, target, load_sem.at[index])
        for index, (source, target) in enumerate(
            [
                (order_hbm, order), (tokens_hbm, tokens), (mod_hbm, mod), (gain_hbm, gain),
                (stale_hbm, stale),
                (project_hbm.at[0], project_w.at[:, 0:head]),
                (project_hbm.at[1], project_w.at[:, head : 2 * head]),
                (project_hbm.at[2], project_w.at[:, 2 * head : 3 * head]),
                (output_hbm, output_w),
            ]
        )
    ]
    for load in loads:
        load.start()

    barrier = pltpu.get_barrier_semaphore()

    def greet(device):
        pl.semaphore_signal(barrier, inc=1, device_id=device, device_id_type=MESH)

    @pl.loop(1, GROUP)
    def _(step):
        greet((section, chip(step // SIDE, step % SIDE)))

    def greet_cross(other):
        greet((other, me))
        for dx, dy in ((1, 0), (3, 0), (0, 1), (0, 3)):
            greet((other, chip(dx, dy)))

    @pl.when(is_even)
    def _():
        greet_cross(section + 1)

        @pl.when(jnp.logical_not(is_first))
        def _():
            greet((section - 1, me))

    @pl.when(is_odd)
    def _():
        greet_cross(section - 1)

        @pl.when(has_next)
        def _():
            greet((section + 1, me))

    ends = jnp.logical_or(is_first, jnp.logical_not(has_next))

    @pl.when(ends)
    def _():
        pl.semaphore_wait(barrier, GROUP - 1 + 5)

    @pl.when(jnp.logical_not(ends))
    def _():
        pl.semaphore_wait(barrier, GROUP - 1 + 6)

    for load in loads[:4]:
        load.wait()

    @pl.when(is_odd)
    def _():
        send(mod, next_mod, mod_sem.at[0], mod_sem.at[1], (section - 1, me))

    own_slot = jnp.where(y < 2, y, 2 + x // 2)

    def feed(patch):
        first[patch] = tokens[order[patch]]

        def spread(mates):
            incoming[patch, block(own_slot), :] = first[patch]
            for dx, dy in mates:
                send(first.at[patch], incoming.at[patch, block(own_slot), :],
                     token_sent.at[patch], incoming_sem.at[patch, own_slot],
                     (section, chip(dx, dy)))

        @pl.when(y < 2)
        def _():
            spread(((2, 1), (2, 3), (0, 2)))

        @pl.when(y >= 2)
        def _():
            spread(((1, 2), (3, 2), (2, 0)))

    def to_neighbours(patch, slot, part, start, target_section, sent):
        along = ((1, 0), (3, 0)) if slot < 2 else ((0, 1), (0, 3))
        across = ((0, 1), (0, 3)) if slot < 2 else ((1, 0), (3, 0))
        for dx, dy in (*along, across[slot % 2]):
            send(part, land.at[patch, pl.ds(start, rows), :], sent,
                 land_sem.at[patch, slot // 2], (target_section, chip(dx, dy)))

    def held_block(slot):
        return pl.multiple_of(held_start(x, y, slot // 2) + (slot % 2) * rows, rows)

    def exchange(patch):
        for slot in range(HELD):
            arrived = incoming.at[patch, pl.ds(slot * rows, rows), :]

            @pl.when(jnp.logical_or(jnp.logical_not(is_first), own_slot != slot))
            def _():
                wait(arrived, incoming_sem.at[patch, slot])

            start = held_block(slot)
            part = land.at[patch, pl.ds(start, rows), :]
            land[patch, pl.ds(start, rows), :] = normalized(
                arrived[...].astype(jnp.float32), mod[0], mod[1]
            )
            to_neighbours(patch, slot, part, start, section, land_sent.at[patch])

        @pl.when(jnp.logical_and(is_first, patch < patches - 1))
        def _():
            feed(patch + 1)

    def spot_of(place):
        spot = jnp.int32(0)
        for t in range(1, patches):
            spot = jnp.where(order[t] == place, t, spot)
        return spot

    @pl.when(is_first)
    def _():
        feed(0)

    @pl.when(is_even)
    def _():
        exchange(0)

    loads[4].wait()
    for patch in range(1, patches):
        place = pl.ds(patch * patch_rows, patch_rows)
        key_unit[place, :] = unit_rows(stale[0, order[patch]], gain[1:2, :]).astype(jnp.bfloat16)
        value_rows[place, :] = stale[1, order[patch]]

    for load in loads[5:8]:
        load.wait()

    def attend(patch):
        parts = []
        for kind in range(2):
            @pl.when(is_even)
            def _():
                wait(land.at[patch, pl.ds(0, 6 * rows), :], land_sem.at[patch, kind])

            @pl.when(is_odd)
            def _():
                wait(land.at[patch, pl.ds(0, 8 * rows), :], land_sem.at[patch, kind])

            parts.append(
                jnp.dot(
                    land[patch, kind * 8 * rows : (kind + 1) * 8 * rows, :], project_w[...],
                    preferred_element_type=jnp.float32,
                ).astype(jnp.bfloat16)
            )
        projected = jnp.concatenate(parts, axis=0)
        place = pl.ds(pl.multiple_of(patch * patch_rows, patch_rows), patch_rows)
        keys, values = projected[:, head : 2 * head], projected[:, 2 * head :]
        key_unit[place, :] = unit_rows(keys, gain[1:2, :]).astype(jnp.bfloat16)
        value_rows[place, :] = values
        query_unit = (
            unit_rows(projected[:, :head], gain[0:1, :]) / math.sqrt(head)
        ).astype(jnp.bfloat16)
        scores = lax.dot_general(
            query_unit, key_unit[...], (((1,), (1,)), ((), ())),
            preferred_element_type=jnp.float32,
        )
        exp_scores = jnp.exp(scores)
        denominator = jnp.sum(exp_scores, axis=-1, keepdims=True)
        summed = jnp.dot(
            exp_scores.astype(jnp.bfloat16), value_rows[...], preferred_element_type=jnp.float32
        )
        attended[patch] = (summed / denominator).astype(jnp.bfloat16)
        own_columns = pl.ds(pl.multiple_of(me * head, head), head)

        @pl.loop(0, GROUP - 1)
        def _(step):
            dx, dy = (GROUP - 1 - step) // SIDE, (GROUP - 1 - step) % SIDE
            to_x, to_y = (x + dx) % SIDE, (y + dy) % SIDE
            for kind in range(2):
                send(attended.at[patch, pl.ds(held_start(to_x, to_y, kind), 2 * rows), :],
                     heads_land.at[patch, pl.ds(kind * 2 * rows, 2 * rows), own_columns],
                     head_sent.at[patch], head_sem.at[patch, (SIDE - dx) % SIDE],
                     (section, to_x * SIDE + to_y))

        for kind in range(2):
            heads_land[patch, kind * 2 * rows : (kind + 1) * 2 * rows, own_columns] = attended[
                patch, pl.ds(held_start(x, y, kind), 2 * rows), :
            ]
        for index, spot in enumerate(BLOCK_ORDER):
            taken = slice(index * rows, (index + 1) * rows)
            fresh[0, patch, spot * rows : (spot + 1) * rows, :] = keys[taken]
            fresh[1, patch, spot * rows : (spot + 1) * rows, :] = values[taken]

        @pl.when(patch == patches - 1)
        def _():
            for place in range(patches):
                cache_ref[0, place] = fresh[0, spot_of(place)]
                cache_ref[1, place] = fresh[1, spot_of(place)]

    def finish(patch):
        half = width // 2

        @pl.loop(0, SIDE)
        def _(step):
            gap = step + step // 2 - 2 * (step // 3)
            columns = pl.ds(
                pl.multiple_of(((x + gap) % SIDE) * (SIDE * head), SIDE * head), SIDE * head
            )

            @pl.when(step == 0)
            def _():
                wait(heads_land.at[patch, :, pl.ds(0, (SIDE - 1) * head)],
                     head_sem.at[patch, 0])
                total[...] = jnp.zeros_like(total)

            @pl.when(step > 0)
            def _():
                wait(heads_land.at[patch, :, pl.ds(0, SIDE * head)], head_sem.at[patch, gap])

            for start in range(0, width, half):
                total[:, start : start + half] += jnp.dot(
                    heads_land[patch, :, columns], output_w[columns, start : start + half],
                    preferred_element_type=jnp.float32,
                )

        @pl.when(is_odd)
        def _():
            for slot in range(HELD):
                wait(incoming.at[patch, pl.ds(slot * rows, rows), :],
                     incoming_sem.at[patch, slot])

        @pl.when(jnp.logical_and(is_even, patch == 0))
        def _():
            wait(next_mod, mod_sem.at[1])

        for slot in range(HELD):
            taken = pl.ds(slot * rows, rows)
            produced[patch, taken, :] = (
                incoming[patch, taken, :].astype(jnp.float32) + mod[2] * total[taken, :]
            ).astype(jnp.bfloat16)

            @pl.when(is_even)
            def _():
                start = held_block(slot)
                part = normed.at[patch, taken, :]
                normed[patch, taken, :] = normalized(
                    produced[patch, taken, :].astype(jnp.float32), next_mod[0], next_mod[1]
                )
                to_neighbours(patch, slot, part, start, section + 1, normed_sent.at[patch])
                send(part, land.at[patch, pl.ds(start, rows), :], normed_sent.at[patch],
                     land_sem.at[patch, slot // 2], (section + 1, me))

            @pl.when(has_next)
            def _():
                send(produced.at[patch, taken, :], incoming.at[patch, taken, :],
                     produced_sent.at[patch], incoming_sem.at[patch, slot], (section + 1, me))

        results[patch] = produced[patch, block(own_slot), :]

        @pl.when(patch == patches - 1)
        def _():
            for place in range(patches):
                out_ref[place] = results[spot_of(place)]

    @pl.loop(0, patches)
    def _(patch):
        attend(patch)

        @pl.when(jnp.logical_and(is_even, patch < patches - 1))
        def _():
            exchange(patch + 1)

        @pl.when(patch == 0)
        def _():
            loads[8].wait()

        finish(patch)

    @pl.when(is_odd)
    def _():
        wait(next_mod, mod_sem.at[0])

    @pl.loop(0, patches)
    def _(patch):
        wait(heads_land.at[patch, :, pl.ds(0, (GROUP - 1) * head)], head_sent.at[patch])

        @pl.when(is_even)
        def _():
            wait(land.at[patch, pl.ds(0, 3 * HELD * rows), :], land_sent.at[patch])
            wait(land.at[patch], normed_sent.at[patch])

        @pl.when(is_first)
        def _():
            wait(incoming.at[patch, pl.ds(0, 3 * rows), :], token_sent.at[patch])

        @pl.when(has_next)
        def _():
            wait(produced.at[patch], produced_sent.at[patch])


def body(
    patch_tokens, patch_order, modulation, norm_gain, project_weight, output_weight, stale_cache
):
    sections = lax.axis_size("section")
    patches, rows, width = patch_tokens.shape
    head = project_weight.shape[-1]
    patch_rows = rows * GROUP
    tokens = patches * patch_rows
    columns = project_weight.reshape(width, 3, head).transpose(1, 0, 2)
    vmem, hbm = pl.BlockSpec(memory_space=pltpu.VMEM), pl.BlockSpec(memory_space=pl.ANY)
    bf16, f32, dma = jnp.bfloat16, jnp.float32, pltpu.SemaphoreType.DMA
    results, cache = pl.pallas_call(
        functools.partial(kernel, sections, patches, rows, width, head),
        out_shape=(
            jax.ShapeDtypeStruct((patches, rows, width), bf16),
            jax.ShapeDtypeStruct((2, patches, patch_rows, head), bf16),
        ),
        in_specs=[hbm] * 7,
        out_specs=(vmem, vmem),
        scratch_shapes=[
            pltpu.SMEM((patches,), jnp.int32),
            pltpu.VMEM((patches, rows, width), bf16),
            pltpu.VMEM((3, 1, width), f32),
            pltpu.VMEM((2, head), f32),
            pltpu.VMEM((2, patches, patch_rows, head), bf16),
            pltpu.VMEM((width, 3 * head), bf16),
            pltpu.VMEM((GROUP * head, width), bf16),
            pltpu.VMEM((patches, rows, width), bf16),
            pltpu.VMEM((patches, HELD * rows, width), bf16),
            pltpu.VMEM((patches, HELD * rows, width), bf16),
            pltpu.VMEM((patches, patch_rows, width), bf16),
            pltpu.VMEM((patches, patch_rows, head), bf16),
            pltpu.VMEM((patches, HELD * rows, GROUP * head), bf16),
            pltpu.VMEM((tokens, head), bf16),
            pltpu.VMEM((tokens, head), bf16),
            pltpu.VMEM((HELD * rows, width), f32),
            pltpu.VMEM((patches, rows, width), bf16),
            pltpu.VMEM((2, patches, patch_rows, head), bf16),
            pltpu.VMEM((3, 1, width), f32),
            pltpu.VMEM((patches, HELD * rows, width), bf16),
            dma((2,)), dma((patches,)),
            dma((9,)), dma((patches,)), dma((patches, HELD)), dma((patches,)), dma((patches, 2)),
            dma((patches,)), dma((patches, SIDE)), dma((patches,)),
        ],
        compiler_params=pltpu.CompilerParams(
            collective_id=0, has_side_effects=True, vmem_limit_bytes=58 << 20
        ),
        name="blocks",
    )(
        patch_tokens, patch_order, modulation.reshape(3, 1, width), norm_gain[0], columns,
        output_weight[0], stale_cache.reshape(2, patches, patch_rows, head),
    )
    return (results[None], cache.reshape(1, 2, patches, patch_rows, 1, head))


def solution(mesh):
    in_specs = (
        P(None, "seq", None),
        P(),
        P("section", None, None),
        P("section", None, None),
        P("section", None, None, "seq", None),
        P("section", None, None),
        P("section", None, None, None, "seq", None),
    )
    out_specs = (P("section", None, "seq", None), P("section", None, None, None, "seq", None))
    return jax.shard_map(body, mesh=mesh, in_specs=in_specs, out_specs=out_specs, check_vma=False)
```

```python
import functools
import math

import jax
import jax.numpy as jnp
from jax import lax
from jax.experimental import pallas as pl
from jax.experimental.pallas import tpu as pltpu
from jax.sharding import PartitionSpec as P

MESH = pl.DeviceIdType.MESH
SIDE = 4
GROUP = SIDE * SIDE
STEPS = sorted(
    ((dx, dy) for dx in range(SIDE) for dy in range(SIDE)),
    key=lambda step: sum(min(s, SIDE - s) for s in step),
)
HOPS = [sum(min(s, SIDE - s) for s in step) for step in STEPS]
RUNS = ((0, 4), (4, 8), (8, 10), (10, 14), (14, 16))
HELD = 4

BLOCK_ORDER = [
    spot
    for colour in range(SIDE)
    for spot in (SIDE * colour, SIDE * ((colour + 2) % SIDE) + 1)
] + [
    SIDE * ((1 if colour < 2 else 0) + 2 * turn) + 2 + colour % 2
    for colour in range(SIDE)
    for turn in range(2)
]


def unit_rows(values, gain):
    floats = values.astype(jnp.float32)
    return floats * lax.rsqrt(jnp.mean(floats * floats, axis=-1, keepdims=True) + 1e-06) * gain


def normalized(values, shift, scale):
    centre = jnp.mean(values, axis=-1, keepdims=True)
    moved = values - centre
    spread_sq = jnp.mean(moved * moved, axis=-1, keepdims=True)
    return (moved * lax.rsqrt(spread_sq + 1e-06) * (1.0 + scale) + shift).astype(jnp.bfloat16)


def kernel(
    sections, patches, rows, width, head,
    tokens_hbm, order_hbm, mod_hbm, gain_hbm, project_hbm, output_hbm, stale_hbm,
    out_ref, cache_ref,
    order, tokens, mod, gain, stale, project_w, output_w, first, incoming, produced, land,
    attended, staged, heads_land, key_unit, value_rows, total, results, fresh,
    next_mod, normed, mod_sem, normed_sent,
    load_sem, token_sent, incoming_sem, produced_sent, land_sem, land_sent, head_sem, head_sent,
):
    section = lax.axis_index("section")
    me = lax.axis_index("seq")
    x, y = me // SIDE, me % SIDE
    patch_rows = rows * GROUP
    is_first = section == 0
    has_next = section < sections - 1
    is_even = section % 2 == 0
    is_odd = section % 2 == 1

    def chip(dx, dy):
        return ((x + dx) % SIDE) * SIDE + (y + dy) % SIDE

    def held_start(chip_x, chip_y, kind):
        if kind == 0:
            return pl.multiple_of(((chip_x + 2 * chip_y) % SIDE) * (2 * rows), 2 * rows)
        return pl.multiple_of(
            patch_rows // 2 + ((2 * chip_x + chip_y) % SIDE) * (2 * rows), 2 * rows
        )

    def block(index):
        return pl.ds(pl.multiple_of(index * rows, rows), rows)

    def send(source, target, sent, arrived, device):
        pltpu.make_async_remote_copy(
            src_ref=source, dst_ref=target, send_sem=sent, recv_sem=arrived,
            device_id=device, device_id_type=MESH,
        ).start()

    def wait(ref, sem):
        pltpu.make_async_copy(ref, ref, sem).wait()

    loads = [
        pltpu.make_async_copy(source, target, load_sem.at[index])
        for index, (source, target) in enumerate(
            [
                (order_hbm, order), (tokens_hbm, tokens), (mod_hbm, mod), (gain_hbm, gain),
                (stale_hbm, stale),
                (project_hbm.at[0], project_w.at[:, 0:head]),
                (project_hbm.at[1], project_w.at[:, head : 2 * head]),
                (project_hbm.at[2], project_w.at[:, 2 * head : 3 * head]),
                (output_hbm, output_w),
            ]
        )
    ]
    for load in loads:
        load.start()

    barrier = pltpu.get_barrier_semaphore()

    def greet(device):
        pl.semaphore_signal(barrier, inc=1, device_id=device, device_id_type=MESH)

    @pl.loop(1, GROUP)
    def _(step):
        greet((section, chip(step // SIDE, step % SIDE)))

    def greet_cross(other):
        greet((other, me))
        for dx, dy in ((1, 0), (3, 0), (0, 1), (0, 3)):
            greet((other, chip(dx, dy)))

    @pl.when(is_even)
    def _():
        greet_cross(section + 1)

        @pl.when(jnp.logical_not(is_first))
        def _():
            greet((section - 1, me))

    @pl.when(is_odd)
    def _():
        greet_cross(section - 1)

        @pl.when(has_next)
        def _():
            greet((section + 1, me))

    ends = jnp.logical_or(is_first, jnp.logical_not(has_next))

    @pl.when(ends)
    def _():
        pl.semaphore_wait(barrier, GROUP - 1 + 5)

    @pl.when(jnp.logical_not(ends))
    def _():
        pl.semaphore_wait(barrier, GROUP - 1 + 6)

    for load in loads[:4]:
        load.wait()

    @pl.when(is_odd)
    def _():
        send(mod, next_mod, mod_sem.at[0], mod_sem.at[1], (section - 1, me))

    own_slot = jnp.where(y < 2, y, 2 + x // 2)

    def feed(patch):
        first[patch] = tokens[order[patch]]

        def spread(mates):
            incoming[patch, block(own_slot), :] = first[patch]
            for dx, dy in mates:
                send(first.at[patch], incoming.at[patch, block(own_slot), :],
                     token_sent.at[patch], incoming_sem.at[patch, own_slot],
                     (section, chip(dx, dy)))

        @pl.when(y < 2)
        def _():
            spread(((2, 1), (2, 3), (0, 2)))

        @pl.when(y >= 2)
        def _():
            spread(((1, 2), (3, 2), (2, 0)))

    def to_neighbours(patch, slot, part, start, target_section, sent):
        along = ((1, 0), (3, 0)) if slot < 2 else ((0, 1), (0, 3))
        across = ((0, 1), (0, 3)) if slot < 2 else ((1, 0), (3, 0))
        for dx, dy in (*along, across[slot % 2]):
            send(part, land.at[patch, pl.ds(start, rows), :], sent,
                 land_sem.at[patch, slot // 2], (target_section, chip(dx, dy)))

    def held_block(slot):
        return pl.multiple_of(held_start(x, y, slot // 2) + (slot % 2) * rows, rows)

    def exchange(patch):
        for slot in range(HELD):
            arrived = incoming.at[patch, pl.ds(slot * rows, rows), :]

            @pl.when(jnp.logical_or(jnp.logical_not(is_first), own_slot != slot))
            def _():
                wait(arrived, incoming_sem.at[patch, slot])

            start = held_block(slot)
            part = land.at[patch, pl.ds(start, rows), :]
            land[patch, pl.ds(start, rows), :] = normalized(
                arrived[...].astype(jnp.float32), mod[0], mod[1]
            )
            to_neighbours(patch, slot, part, start, section, land_sent.at[patch])

        @pl.when(jnp.logical_and(is_first, patch < patches - 1))
        def _():
            feed(patch + 1)

    def spot_of(place):
        spot = jnp.int32(0)
        for t in range(1, patches):
            spot = jnp.where(order[t] == place, t, spot)
        return spot

    @pl.when(is_first)
    def _():
        feed(0)

    @pl.when(is_even)
    def _():
        exchange(0)

    loads[4].wait()
    for patch in range(1, patches):
        place = pl.ds(patch * patch_rows, patch_rows)
        key_unit[place, :] = unit_rows(stale[0, order[patch]], gain[1:2, :]).astype(jnp.bfloat16)
        value_rows[place, :] = stale[1, order[patch]]

    for load in loads[5:8]:
        load.wait()

    def attend(patch):
        parts = []
        for kind in range(2):
            @pl.when(is_even)
            def _():
                wait(land.at[patch, pl.ds(0, 6 * rows), :], land_sem.at[patch, kind])

            @pl.when(is_odd)
            def _():
                wait(land.at[patch, pl.ds(0, 8 * rows), :], land_sem.at[patch, kind])

            parts.append(
                jnp.dot(
                    land[patch, kind * 8 * rows : (kind + 1) * 8 * rows, :], project_w[...],
                    preferred_element_type=jnp.float32,
                ).astype(jnp.bfloat16)
            )
        projected = jnp.concatenate(parts, axis=0)
        place = pl.ds(pl.multiple_of(patch * patch_rows, patch_rows), patch_rows)
        keys, values = projected[:, head : 2 * head], projected[:, 2 * head :]
        key_unit[place, :] = unit_rows(keys, gain[1:2, :]).astype(jnp.bfloat16)
        value_rows[place, :] = values
        query_unit = (
            unit_rows(projected[:, :head], gain[0:1, :]) / math.sqrt(head)
        ).astype(jnp.bfloat16)
        scores = lax.dot_general(
            query_unit, key_unit[...], (((1,), (1,)), ((), ())),
            preferred_element_type=jnp.float32,
        )
        exp_scores = jnp.exp(scores)
        denominator = jnp.sum(exp_scores, axis=-1, keepdims=True)
        summed = jnp.dot(
            exp_scores.astype(jnp.bfloat16), value_rows[...], preferred_element_type=jnp.float32
        )
        attended[...] = (summed / denominator).astype(jnp.bfloat16)

        for index, (dx, dy) in enumerate(STEPS[1:], 1):
            to_x, to_y = (x + dx) % SIDE, (y + dy) % SIDE
            for kind in range(2):
                staged[patch, index, kind * 2 * rows : (kind + 1) * 2 * rows, :] = (
                    attended[pl.ds(held_start(to_x, to_y, kind), 2 * rows), :]
                )
            seen = STEPS.index(((SIDE - dx) % SIDE, (SIDE - dy) % SIDE))
            send(staged.at[patch, index],
                 heads_land.at[patch, :, seen * head : (seen + 1) * head],
                 head_sent.at[patch], head_sem.at[patch, HOPS[index] - 1],
                 (section, to_x * SIDE + to_y))

        for kind in range(2):
            heads_land[patch, kind * 2 * rows : (kind + 1) * 2 * rows, :head] = attended[
                pl.ds(held_start(x, y, kind), 2 * rows), :
            ]
        for index, spot in enumerate(BLOCK_ORDER):
            taken = slice(index * rows, (index + 1) * rows)
            fresh[0, patch, spot * rows : (spot + 1) * rows, :] = keys[taken]
            fresh[1, patch, spot * rows : (spot + 1) * rows, :] = values[taken]

        @pl.when(patch == patches - 1)
        def _():
            for place in range(patches):
                cache_ref[0, place] = fresh[0, spot_of(place)]
                cache_ref[1, place] = fresh[1, spot_of(place)]

    def finish(patch):
        arrived = 0
        for begin, end in RUNS:
            while arrived < HOPS[end - 1]:
                arrived += 1
                wait(heads_land.at[patch, :, pl.ds(0, HOPS.count(arrived) * head)],
                     head_sem.at[patch, arrived - 1])
            weights = jnp.concatenate(
                [
                    output_w[pl.ds(pl.multiple_of(chip(dx, dy) * head, head), head), :]
                    for dx, dy in STEPS[begin:end]
                ],
                axis=0,
            )
            product = jnp.dot(
                heads_land[patch, :, begin * head : end * head], weights,
                preferred_element_type=jnp.float32,
            )
            total[...] = product if begin == 0 else total[...] + product

        @pl.when(is_odd)
        def _():
            wait(incoming.at[patch], incoming_sem.at[patch, 0])

        @pl.when(jnp.logical_and(is_even, patch == 0))
        def _():
            wait(next_mod, mod_sem.at[1])

        for slot in range(HELD):
            taken = pl.ds(slot * rows, rows)
            produced[patch, taken, :] = (
                incoming[patch, taken, :].astype(jnp.float32) + mod[2] * total[taken, :]
            ).astype(jnp.bfloat16)

            @pl.when(is_even)
            def _():
                part = normed.at[patch, taken, :]
                normed[patch, taken, :] = normalized(
                    produced[patch, taken, :].astype(jnp.float32), next_mod[0], next_mod[1]
                )
                to_neighbours(
                    patch, slot, part, held_block(slot), section + 1, normed_sent.at[patch]
                )

            @pl.when(jnp.logical_and(is_odd, has_next))
            def _():
                send(produced.at[patch, taken, :], incoming.at[patch, taken, :],
                     produced_sent.at[patch], incoming_sem.at[patch, slot], (section + 1, me))

        @pl.when(is_even)
        def _():
            for kind in range(2):
                send(normed.at[patch, pl.ds(kind * 2 * rows, 2 * rows), :],
                     land.at[patch, pl.ds(held_start(x, y, kind), 2 * rows), :],
                     normed_sent.at[patch], land_sem.at[patch, kind], (section + 1, me))
            send(produced.at[patch], incoming.at[patch],
                 produced_sent.at[patch], incoming_sem.at[patch, 0], (section + 1, me))

        results[patch] = produced[patch, block(own_slot), :]

        @pl.when(patch == patches - 1)
        def _():
            for place in range(patches):
                out_ref[place] = results[spot_of(place)]

    @pl.loop(0, patches)
    def _(patch):
        attend(patch)

        @pl.when(jnp.logical_and(is_even, patch < patches - 1))
        def _():
            exchange(patch + 1)

        @pl.when(patch == 0)
        def _():
            loads[8].wait()

        finish(patch)

    @pl.when(is_odd)
    def _():
        wait(next_mod, mod_sem.at[0])

    @pl.loop(0, patches)
    def _(patch):
        wait(heads_land.at[patch, :, pl.ds(0, (GROUP - 1) * head)], head_sent.at[patch])

        @pl.when(is_even)
        def _():
            wait(land.at[patch, pl.ds(0, 3 * HELD * rows), :], land_sent.at[patch])
            wait(land.at[patch], normed_sent.at[patch])

        @pl.when(is_first)
        def _():
            wait(incoming.at[patch, pl.ds(0, 3 * rows), :], token_sent.at[patch])

        @pl.when(has_next)
        def _():
            wait(produced.at[patch], produced_sent.at[patch])


def copy_kernel(out_ref, cache_ref, out_to, cache_to, out_held, cache_held, sem):
    pieces = [
        (held.at[part], source.at[part], target.at[part], index, part)
        for index, (held, source, target) in enumerate(
            ((cache_held, cache_ref, cache_to), (out_held, out_ref, out_to))
        )
        for part in range(source.shape[0])
    ]
    inward = [
        pltpu.make_async_copy(source, held, sem.at[0, index, part])
        for held, source, _, index, part in pieces
    ]
    outward = [
        pltpu.make_async_copy(held, target, sem.at[1, index, part])
        for held, _, target, index, part in pieces
    ]
    for copy in inward:
        copy.start()
    for copy, onward in zip(inward, outward):
        copy.wait()
        onward.start()
    for copy in outward:
        copy.wait()


def body(
    patch_tokens, patch_order, modulation, norm_gain, project_weight, output_weight, stale_cache
):
    sections = lax.axis_size("section")
    patches, rows, width = patch_tokens.shape
    head = project_weight.shape[-1]
    patch_rows = rows * GROUP
    tokens = patches * patch_rows
    columns = project_weight.reshape(width, 3, head).transpose(1, 0, 2)
    vmem, hbm = pl.BlockSpec(memory_space=pltpu.VMEM), pl.BlockSpec(memory_space=pltpu.HBM)
    bf16, f32, dma = jnp.bfloat16, jnp.float32, pltpu.SemaphoreType.DMA
    shapes = (
        jax.ShapeDtypeStruct((patches, rows, width), jnp.bfloat16),
        jax.ShapeDtypeStruct((2, patches, patch_rows, head), jnp.bfloat16),
    )
    results, cache = pl.pallas_call(
        functools.partial(kernel, sections, patches, rows, width, head),
        out_shape=shapes,
        in_specs=[hbm] * 7,
        out_specs=(vmem, vmem),
        scratch_shapes=[
            pltpu.SMEM((patches,), jnp.int32),
            pltpu.VMEM((patches, rows, width), bf16),
            pltpu.VMEM((3, 1, width), f32),
            pltpu.VMEM((2, head), f32),
            pltpu.VMEM((2, patches, patch_rows, head), bf16),
            pltpu.VMEM((width, 3 * head), bf16),
            pltpu.VMEM((GROUP * head, width), bf16),
            pltpu.VMEM((patches, rows, width), bf16),
            pltpu.VMEM((patches, HELD * rows, width), bf16),
            pltpu.VMEM((patches, HELD * rows, width), bf16),
            pltpu.VMEM((patches, patch_rows, width), bf16),
            pltpu.VMEM((patch_rows, head), bf16),
            pltpu.VMEM((patches, GROUP, HELD * rows, head), bf16),
            pltpu.VMEM((patches, HELD * rows, GROUP * head), bf16),
            pltpu.VMEM((tokens, head), bf16),
            pltpu.VMEM((tokens, head), bf16),
            pltpu.VMEM((HELD * rows, width), f32),
            pltpu.VMEM((patches, rows, width), bf16),
            pltpu.VMEM((2, patches, patch_rows, head), bf16),
            pltpu.VMEM((3, 1, width), f32),
            pltpu.VMEM((patches, HELD * rows, width), bf16),
            dma((2,)), dma((patches,)),
            dma((9,)), dma((patches,)), dma((patches, HELD)), dma((patches,)), dma((patches, 2)),
            dma((patches,)), dma((patches, SIDE)), dma((patches,)),
        ],
        compiler_params=pltpu.CompilerParams(
            collective_id=0, has_side_effects=True, vmem_limit_bytes=58 << 20
        ),
        name="blocks",
    )(
        patch_tokens, patch_order, modulation.reshape(3, 1, width), norm_gain[0], columns,
        output_weight[0], stale_cache.reshape(2, patches, patch_rows, head),
    )
    results, cache = pl.pallas_call(
        copy_kernel,
        out_shape=shapes,
        in_specs=[hbm] * 2,
        out_specs=(hbm, hbm),
        scratch_shapes=[
            pltpu.VMEM((patches, rows, width), bf16),
            pltpu.VMEM((2, patches, patch_rows, head), bf16),
            dma((2, 2, patches)),
        ],
        name="results",
    )(results, cache)
    return (results[None], cache.reshape(1, 2, patches, patch_rows, 1, head))


def solution(mesh):
    in_specs = (
        P(None, "seq", None),
        P(),
        P("section", None, None),
        P("section", None, None),
        P("section", None, None, "seq", None),
        P("section", None, None),
        P("section", None, None, None, "seq", None),
    )
    out_specs = (P("section", None, "seq", None), P("section", None, None, None, "seq", None))
    return jax.shard_map(body, mesh=mesh, in_specs=in_specs, out_specs=out_specs, check_vma=False)
```

```python
import functools
import math

import jax
import jax.numpy as jnp
from jax import lax
from jax.experimental import pallas as pl
from jax.experimental.pallas import tpu as pltpu
from jax.sharding import PartitionSpec as P

MESH = pl.DeviceIdType.MESH
SIDE = 4
GROUP = SIDE * SIDE
STEPS = sorted(
    ((dx, dy) for dx in range(SIDE) for dy in range(SIDE)),
    key=lambda step: sum(min(s, SIDE - s) for s in step),
)
HOPS = [sum(min(s, SIDE - s) for s in step) for step in STEPS]
RUNS = ((0, 4), (4, 8), (8, 10), (10, 14), (14, 16))
HELD = 4

BLOCK_ORDER = [
    spot
    for colour in range(SIDE)
    for spot in (SIDE * colour, SIDE * ((colour + 2) % SIDE) + 1)
] + [
    SIDE * ((1 if colour < 2 else 0) + 2 * turn) + 2 + colour % 2
    for colour in range(SIDE)
    for turn in range(2)
]


def unit_rows(values, gain):
    floats = values.astype(jnp.float32)
    return floats * lax.rsqrt(jnp.mean(floats * floats, axis=-1, keepdims=True) + 1e-06) * gain


def normalized(values, shift, scale):
    centre = jnp.mean(values, axis=-1, keepdims=True)
    moved = values - centre
    spread_sq = jnp.mean(moved * moved, axis=-1, keepdims=True)
    return (moved * lax.rsqrt(spread_sq + 1e-06) * (1.0 + scale) + shift).astype(jnp.bfloat16)


def kernel(
    sections, patches, rows, width, head,
    tokens_hbm, order_hbm, mod_hbm, gain_hbm, project_hbm, output_hbm, stale_hbm,
    out_ref, cache_ref,
    order, tokens, mod, gain, stale, project_w, output_w, first, incoming, produced, land,
    attended, staged, heads_land, key_unit, value_rows, total, results, fresh,
    next_mod, normed, mod_sem, normed_sent, early_sem, early_sent,
    load_sem, token_sent, incoming_sem, produced_sent, land_sem, land_sent, head_sem, head_sent,
):
    section = lax.axis_index("section")
    me = lax.axis_index("seq")
    x, y = me // SIDE, me % SIDE
    patch_rows = rows * GROUP
    is_first = section == 0
    has_next = section < sections - 1
    is_helper = section == sections - 2
    is_even = section % 2 == 0
    is_odd = section % 2 == 1

    def chip(dx, dy):
        return ((x + dx) % SIDE) * SIDE + (y + dy) % SIDE

    def held_start(chip_x, chip_y, kind):
        if kind == 0:
            return pl.multiple_of(((chip_x + 2 * chip_y) % SIDE) * (2 * rows), 2 * rows)
        return pl.multiple_of(
            patch_rows // 2 + ((2 * chip_x + chip_y) % SIDE) * (2 * rows), 2 * rows
        )

    def block(index):
        return pl.ds(pl.multiple_of(index * rows, rows), rows)

    def send(source, target, sent, arrived, device):
        pltpu.make_async_remote_copy(
            src_ref=source, dst_ref=target, send_sem=sent, recv_sem=arrived,
            device_id=device, device_id_type=MESH,
        ).start()

    def wait(ref, sem):
        pltpu.make_async_copy(ref, ref, sem).wait()

    loads = [
        pltpu.make_async_copy(source, target, load_sem.at[index])
        for index, (source, target) in enumerate(
            [
                (order_hbm, order), (tokens_hbm, tokens), (mod_hbm, mod), (gain_hbm, gain),
                (stale_hbm, stale),
                (project_hbm.at[0], project_w.at[:, 0:head]),
                (project_hbm.at[1], project_w.at[:, head : 2 * head]),
                (project_hbm.at[2], project_w.at[:, 2 * head : 3 * head]),
                (output_hbm, output_w),
            ]
        )
    ]
    for load in loads:
        load.start()

    barrier = pltpu.get_barrier_semaphore()

    def greet(device):
        pl.semaphore_signal(barrier, inc=1, device_id=device, device_id_type=MESH)

    @pl.loop(1, GROUP)
    def _(step):
        greet((section, chip(step // SIDE, step % SIDE)))

    def greet_cross(other):
        greet((other, me))
        for dx, dy in ((1, 0), (3, 0), (0, 1), (0, 3)):
            greet((other, chip(dx, dy)))

    @pl.when(is_even)
    def _():
        greet_cross(section + 1)

        @pl.when(jnp.logical_not(is_first))
        def _():
            greet((section - 1, me))

        @pl.when(is_first)
        def _():
            greet((sections - 2, me))

        @pl.when(is_helper)
        def _():
            greet((0, me))

    @pl.when(is_odd)
    def _():
        greet_cross(section - 1)

        @pl.when(has_next)
        def _():
            greet((section + 1, me))

    @pl.when(is_helper)
    def _():
        pl.semaphore_wait(barrier, GROUP - 1 + 7)

    @pl.when(jnp.logical_not(has_next))
    def _():
        pl.semaphore_wait(barrier, GROUP - 1 + 5)

    @pl.when(jnp.logical_and(has_next, jnp.logical_not(is_helper)))
    def _():
        pl.semaphore_wait(barrier, GROUP - 1 + 6)

    for load in loads[:4]:
        load.wait()

    @pl.when(is_odd)
    def _():
        send(mod, next_mod, mod_sem.at[0], mod_sem.at[1], (section - 1, me))

    own_slot = jnp.where(y < 2, y, 2 + x // 2)

    def feed(patch, held, arrived):
        def spread(mates):
            for dx, dy in mates:
                send(first.at[patch], held.at[patch, block(own_slot), :],
                     token_sent.at[patch], arrived.at[patch, own_slot],
                     (section, chip(dx, dy)))

        @pl.when(y < 2)
        def _():
            spread(((2, 1), (2, 3), (0, 2)))

        @pl.when(y >= 2)
        def _():
            spread(((1, 2), (3, 2), (2, 0)))

    def to_neighbours(patch, slot, part, start, target_section, sent):
        along = ((1, 0), (3, 0)) if slot < 2 else ((0, 1), (0, 3))
        across = ((0, 1), (0, 3)) if slot < 2 else ((1, 0), (3, 0))
        for dx, dy in (*along, across[slot % 2]):
            send(part, land.at[patch, pl.ds(start, rows), :], sent,
                 land_sem.at[patch, slot // 2], (target_section, chip(dx, dy)))

    def held_block(slot):
        return pl.multiple_of(held_start(x, y, slot // 2) + (slot % 2) * rows, rows)

    def exchange(patch):
        for slot in range(HELD):
            arrived = incoming.at[patch, pl.ds(slot * rows, rows), :]

            @pl.when(jnp.logical_or(jnp.logical_not(is_first), own_slot != slot))
            def _():
                wait(arrived, incoming_sem.at[patch, slot])

            start = held_block(slot)
            part = land.at[patch, pl.ds(start, rows), :]
            land[patch, pl.ds(start, rows), :] = normalized(
                arrived[...].astype(jnp.float32), mod[0], mod[1]
            )
            to_neighbours(patch, slot, part, start, section, land_sent.at[patch])

    def spot_of(place):
        spot = jnp.int32(0)
        for t in range(1, patches):
            spot = jnp.where(order[t] == place, t, spot)
        return spot

    @pl.when(is_first)
    def _():
        for patch in range(patches):
            first[patch] = tokens[order[patch]]
            incoming[patch, block(own_slot), :] = first[patch]
        feed(0, incoming, incoming_sem)

    @pl.when(is_helper)
    def _():
        for patch in range(1, patches):
            first[patch] = tokens[order[patch]]
            feed(patch, normed, early_sem)
        for patch in range(1, patches):
            for slot in range(HELD):
                @pl.when(own_slot != slot)
                def _():
                    part = normed.at[patch, slot * rows : (slot + 1) * rows, :]
                    wait(part, early_sem.at[patch, slot])
                    send(part, incoming.at[patch, slot * rows : (slot + 1) * rows, :],
                         early_sent.at[patch], incoming_sem.at[patch, slot], (0, me))
        for patch in range(1, patches):
            wait(normed.at[patch, 0 : (HELD - 1) * rows, :], early_sent.at[patch])

    @pl.when(is_even)
    def _():
        exchange(0)

    loads[4].wait()
    for patch in range(1, patches):
        place = pl.ds(patch * patch_rows, patch_rows)
        key_unit[place, :] = unit_rows(stale[0, order[patch]], gain[1:2, :]).astype(jnp.bfloat16)
        value_rows[place, :] = stale[1, order[patch]]

    for load in loads[5:8]:
        load.wait()

    def attend(patch):
        parts = []
        for kind in range(2):
            @pl.when(is_even)
            def _():
                wait(land.at[patch, pl.ds(0, 6 * rows), :], land_sem.at[patch, kind])

            @pl.when(is_odd)
            def _():
                wait(land.at[patch, pl.ds(0, 8 * rows), :], land_sem.at[patch, kind])

            parts.append(
                jnp.dot(
                    land[patch, kind * 8 * rows : (kind + 1) * 8 * rows, :], project_w[...],
                    preferred_element_type=jnp.float32,
                ).astype(jnp.bfloat16)
            )
        projected = jnp.concatenate(parts, axis=0)
        place = pl.ds(pl.multiple_of(patch * patch_rows, patch_rows), patch_rows)
        keys, values = projected[:, head : 2 * head], projected[:, 2 * head :]
        key_unit[place, :] = unit_rows(keys, gain[1:2, :]).astype(jnp.bfloat16)
        value_rows[place, :] = values
        query_unit = (
            unit_rows(projected[:, :head], gain[0:1, :]) / math.sqrt(head)
        ).astype(jnp.bfloat16)
        scores = lax.dot_general(
            query_unit, key_unit[...], (((1,), (1,)), ((), ())),
            preferred_element_type=jnp.float32,
        )
        exp_scores = jnp.exp(scores)
        denominator = jnp.sum(exp_scores, axis=-1, keepdims=True)
        summed = jnp.dot(
            exp_scores.astype(jnp.bfloat16), value_rows[...], preferred_element_type=jnp.float32
        )
        attended[...] = (summed / denominator).astype(jnp.bfloat16)

        for index, (dx, dy) in enumerate(STEPS[1:], 1):
            to_x, to_y = (x + dx) % SIDE, (y + dy) % SIDE
            for kind in range(2):
                staged[patch, index, kind * 2 * rows : (kind + 1) * 2 * rows, :] = (
                    attended[pl.ds(held_start(to_x, to_y, kind), 2 * rows), :]
                )
            seen = STEPS.index(((SIDE - dx) % SIDE, (SIDE - dy) % SIDE))
            send(staged.at[patch, index],
                 heads_land.at[patch, :, seen * head : (seen + 1) * head],
                 head_sent.at[patch], head_sem.at[patch, HOPS[index] - 1],
                 (section, to_x * SIDE + to_y))

        for kind in range(2):
            heads_land[patch, kind * 2 * rows : (kind + 1) * 2 * rows, :head] = attended[
                pl.ds(held_start(x, y, kind), 2 * rows), :
            ]
        for index, spot in enumerate(BLOCK_ORDER):
            taken = slice(index * rows, (index + 1) * rows)
            fresh[0, patch, spot * rows : (spot + 1) * rows, :] = keys[taken]
            fresh[1, patch, spot * rows : (spot + 1) * rows, :] = values[taken]

        @pl.when(patch == patches - 1)
        def _():
            for place in range(patches):
                cache_ref[0, place] = fresh[0, spot_of(place)]
                cache_ref[1, place] = fresh[1, spot_of(place)]

    def finish(patch):
        arrived = 0
        for begin, end in RUNS:
            while arrived < HOPS[end - 1]:
                arrived += 1
                wait(heads_land.at[patch, :, pl.ds(0, HOPS.count(arrived) * head)],
                     head_sem.at[patch, arrived - 1])
            weights = jnp.concatenate(
                [
                    output_w[pl.ds(pl.multiple_of(chip(dx, dy) * head, head), head), :]
                    for dx, dy in STEPS[begin:end]
                ],
                axis=0,
            )
            product = jnp.dot(
                heads_land[patch, :, begin * head : end * head], weights,
                preferred_element_type=jnp.float32,
            )
            total[...] = product if begin == 0 else total[...] + product

        @pl.when(is_odd)
        def _():
            wait(incoming.at[patch], incoming_sem.at[patch, 0])

        @pl.when(jnp.logical_and(is_even, patch == 0))
        def _():
            wait(next_mod, mod_sem.at[1])

        for slot in range(HELD):
            taken = pl.ds(slot * rows, rows)
            produced[patch, taken, :] = (
                incoming[patch, taken, :].astype(jnp.float32) + mod[2] * total[taken, :]
            ).astype(jnp.bfloat16)

            @pl.when(is_even)
            def _():
                part = normed.at[patch, taken, :]
                normed[patch, taken, :] = normalized(
                    produced[patch, taken, :].astype(jnp.float32), next_mod[0], next_mod[1]
                )
                to_neighbours(
                    patch, slot, part, held_block(slot), section + 1, normed_sent.at[patch]
                )

            @pl.when(jnp.logical_and(is_odd, has_next))
            def _():
                send(produced.at[patch, taken, :], incoming.at[patch, taken, :],
                     produced_sent.at[patch], incoming_sem.at[patch, slot], (section + 1, me))

        @pl.when(is_even)
        def _():
            for kind in range(2):
                send(normed.at[patch, pl.ds(kind * 2 * rows, 2 * rows), :],
                     land.at[patch, pl.ds(held_start(x, y, kind), 2 * rows), :],
                     normed_sent.at[patch], land_sem.at[patch, kind], (section + 1, me))
            send(produced.at[patch], incoming.at[patch],
                 produced_sent.at[patch], incoming_sem.at[patch, 0], (section + 1, me))

        results[patch] = produced[patch, block(own_slot), :]

        @pl.when(patch == patches - 1)
        def _():
            for place in range(patches):
                out_ref[place] = results[spot_of(place)]

    @pl.loop(0, patches)
    def _(patch):
        attend(patch)

        @pl.when(jnp.logical_and(is_even, patch < patches - 1))
        def _():
            exchange(patch + 1)

        @pl.when(patch == 0)
        def _():
            loads[8].wait()

        finish(patch)

    @pl.when(is_odd)
    def _():
        wait(next_mod, mod_sem.at[0])

    @pl.loop(0, patches)
    def _(patch):
        wait(heads_land.at[patch, :, pl.ds(0, (GROUP - 1) * head)], head_sent.at[patch])

        @pl.when(is_even)
        def _():
            wait(land.at[patch, pl.ds(0, 3 * HELD * rows), :], land_sent.at[patch])
            wait(land.at[patch], normed_sent.at[patch])

        @pl.when(
            jnp.logical_or(
                jnp.logical_and(is_first, patch == 0), jnp.logical_and(is_helper, patch > 0)
            )
        )
        def _():
            wait(incoming.at[patch, pl.ds(0, 3 * rows), :], token_sent.at[patch])

        @pl.when(has_next)
        def _():
            wait(produced.at[patch], produced_sent.at[patch])


def copy_kernel(out_ref, cache_ref, out_to, cache_to, out_held, cache_held, sem):
    pieces = [
        (held.at[part], source.at[part], target.at[part], index, part)
        for index, (held, source, target) in enumerate(
            ((cache_held, cache_ref, cache_to), (out_held, out_ref, out_to))
        )
        for part in range(source.shape[0])
    ]
    inward = [
        pltpu.make_async_copy(source, held, sem.at[0, index, part])
        for held, source, _, index, part in pieces
    ]
    outward = [
        pltpu.make_async_copy(held, target, sem.at[1, index, part])
        for held, _, target, index, part in pieces
    ]
    for copy in inward:
        copy.start()
    for copy, onward in zip(inward, outward):
        copy.wait()
        onward.start()
    for copy in outward:
        copy.wait()


def body(
    patch_tokens, patch_order, modulation, norm_gain, project_weight, output_weight, stale_cache
):
    sections = lax.axis_size("section")
    patches, rows, width = patch_tokens.shape
    head = project_weight.shape[-1]
    patch_rows = rows * GROUP
    tokens = patches * patch_rows
    columns = project_weight.reshape(width, 3, head).transpose(1, 0, 2)
    vmem, hbm = pl.BlockSpec(memory_space=pltpu.VMEM), pl.BlockSpec(memory_space=pltpu.HBM)
    bf16, f32, dma = jnp.bfloat16, jnp.float32, pltpu.SemaphoreType.DMA
    shapes = (
        jax.ShapeDtypeStruct((patches, rows, width), jnp.bfloat16),
        jax.ShapeDtypeStruct((2, patches, patch_rows, head), jnp.bfloat16),
    )
    results, cache = pl.pallas_call(
        functools.partial(kernel, sections, patches, rows, width, head),
        out_shape=shapes,
        in_specs=[hbm] * 7,
        out_specs=(vmem, vmem),
        scratch_shapes=[
            pltpu.SMEM((patches,), jnp.int32),
            pltpu.VMEM((patches, rows, width), bf16),
            pltpu.VMEM((3, 1, width), f32),
            pltpu.VMEM((2, head), f32),
            pltpu.VMEM((2, patches, patch_rows, head), bf16),
            pltpu.VMEM((width, 3 * head), bf16),
            pltpu.VMEM((GROUP * head, width), bf16),
            pltpu.VMEM((patches, rows, width), bf16),
            pltpu.VMEM((patches, HELD * rows, width), bf16),
            pltpu.VMEM((patches, HELD * rows, width), bf16),
            pltpu.VMEM((patches, patch_rows, width), bf16),
            pltpu.VMEM((patch_rows, head), bf16),
            pltpu.VMEM((patches, GROUP, HELD * rows, head), bf16),
            pltpu.VMEM((patches, HELD * rows, GROUP * head), bf16),
            pltpu.VMEM((tokens, head), bf16),
            pltpu.VMEM((tokens, head), bf16),
            pltpu.VMEM((HELD * rows, width), f32),
            pltpu.VMEM((patches, rows, width), bf16),
            pltpu.VMEM((2, patches, patch_rows, head), bf16),
            pltpu.VMEM((3, 1, width), f32),
            pltpu.VMEM((patches, HELD * rows, width), bf16),
            dma((2,)), dma((patches,)), dma((patches, HELD)), dma((patches,)),
            dma((9,)), dma((patches,)), dma((patches, HELD)), dma((patches,)), dma((patches, 2)),
            dma((patches,)), dma((patches, SIDE)), dma((patches,)),
        ],
        compiler_params=pltpu.CompilerParams(
            collective_id=0, has_side_effects=True, vmem_limit_bytes=58 << 20
        ),
        name="blocks",
    )(
        patch_tokens, patch_order, modulation.reshape(3, 1, width), norm_gain[0], columns,
        output_weight[0], stale_cache.reshape(2, patches, patch_rows, head),
    )
    results, cache = pl.pallas_call(
        copy_kernel,
        out_shape=shapes,
        in_specs=[hbm] * 2,
        out_specs=(hbm, hbm),
        scratch_shapes=[
            pltpu.VMEM((patches, rows, width), bf16),
            pltpu.VMEM((2, patches, patch_rows, head), bf16),
            dma((2, 2, patches)),
        ],
        name="results",
    )(results, cache)
    return (results[None], cache.reshape(1, 2, patches, patch_rows, 1, head))


def solution(mesh):
    in_specs = (
        P(None, "seq", None),
        P(),
        P("section", None, None),
        P("section", None, None),
        P("section", None, None, "seq", None),
        P("section", None, None),
        P("section", None, None, None, "seq", None),
    )
    out_specs = (P("section", None, "seq", None), P("section", None, None, None, "seq", None))
    return jax.shard_map(body, mesh=mesh, in_specs=in_specs, out_specs=out_specs, check_vma=False)
```

```python
import functools
import math

import jax
import jax.numpy as jnp
from jax import lax
from jax.experimental import pallas as pl
from jax.experimental.pallas import tpu as pltpu
from jax.sharding import PartitionSpec as P

MESH = pl.DeviceIdType.MESH
SIDE = 4
GROUP = SIDE * SIDE
STEPS = sorted(
    ((dx, dy) for dx in range(SIDE) for dy in range(SIDE)),
    key=lambda step: sum(min(s, SIDE - s) for s in step),
)
HOPS = [sum(min(s, SIDE - s) for s in step) for step in STEPS]
RUNS = ((0, 4), (4, 8), (8, 10), (10, 14), (14, 16))
HELD = 4

BLOCK_ORDER = [
    spot
    for colour in range(SIDE)
    for spot in (SIDE * colour, SIDE * ((colour + 2) % SIDE) + 1)
] + [
    SIDE * ((1 if colour < 2 else 0) + 2 * turn) + 2 + colour % 2
    for colour in range(SIDE)
    for turn in range(2)
]


def unit_rows(values, gain):
    floats = values.astype(jnp.float32)
    return floats * lax.rsqrt(jnp.mean(floats * floats, axis=-1, keepdims=True) + 1e-06) * gain


def normalized(values, shift, scale):
    centre = jnp.mean(values, axis=-1, keepdims=True)
    moved = values - centre
    spread_sq = jnp.mean(moved * moved, axis=-1, keepdims=True)
    return (moved * lax.rsqrt(spread_sq + 1e-06) * (1.0 + scale) + shift).astype(jnp.bfloat16)


def kernel(
    sections, patches, rows, width, head,
    tokens_hbm, order_hbm, mod_hbm, gain_hbm, project_hbm, output_hbm, stale_hbm,
    out_ref, cache_ref,
    order, tokens, mod, gain, stale, project_w, output_w, first, incoming, produced, land,
    attended, staged, heads_land, key_unit, value_rows, total, results, fresh,
    next_mod, normed, mod_sem, normed_sent, early_sem, early_sent,
    load_sem, token_sent, incoming_sem, produced_sent, land_sem, land_sent, head_sem, head_sent,
):
    section = lax.axis_index("section")
    me = lax.axis_index("seq")
    x, y = me // SIDE, me % SIDE
    patch_rows = rows * GROUP
    is_first = section == 0
    has_next = section < sections - 1
    is_helper = section == sections - 2
    is_even = section % 2 == 0
    is_odd = section % 2 == 1

    def chip(dx, dy):
        return ((x + dx) % SIDE) * SIDE + (y + dy) % SIDE

    def held_start(chip_x, chip_y, kind):
        if kind == 0:
            return pl.multiple_of(((chip_x + 2 * chip_y) % SIDE) * (2 * rows), 2 * rows)
        return pl.multiple_of(
            patch_rows // 2 + ((2 * chip_x + chip_y) % SIDE) * (2 * rows), 2 * rows
        )

    def block(index):
        return pl.ds(pl.multiple_of(index * rows, rows), rows)

    def send(source, target, sent, arrived, device):
        pltpu.make_async_remote_copy(
            src_ref=source, dst_ref=target, send_sem=sent, recv_sem=arrived,
            device_id=device, device_id_type=MESH,
        ).start()

    def wait(ref, sem):
        pltpu.make_async_copy(ref, ref, sem).wait()

    loads = [
        pltpu.make_async_copy(source, target, load_sem.at[index])
        for index, (source, target) in enumerate(
            [
                (order_hbm, order), (tokens_hbm, tokens), (mod_hbm, mod), (gain_hbm, gain),
                (stale_hbm, stale),
                (project_hbm.at[0], project_w.at[:, 0:head]),
                (project_hbm.at[1], project_w.at[:, head : 2 * head]),
                (project_hbm.at[2], project_w.at[:, 2 * head : 3 * head]),
                (output_hbm, output_w),
            ]
        )
    ]
    for load in loads:
        load.start()

    barrier = pltpu.get_barrier_semaphore()

    def greet(device):
        pl.semaphore_signal(barrier, inc=1, device_id=device, device_id_type=MESH)

    @pl.loop(1, GROUP)
    def _(step):
        greet((section, chip(step // SIDE, step % SIDE)))

    def greet_cross(other):
        greet((other, me))
        for dx, dy in ((1, 0), (3, 0), (0, 1), (0, 3)):
            greet((other, chip(dx, dy)))

    @pl.when(is_even)
    def _():
        greet_cross(section + 1)

        @pl.when(jnp.logical_not(is_first))
        def _():
            greet((section - 1, me))

        @pl.when(is_first)
        def _():
            greet((sections - 2, me))

        @pl.when(is_helper)
        def _():
            greet((0, me))

    @pl.when(is_odd)
    def _():
        greet_cross(section - 1)

        @pl.when(has_next)
        def _():
            greet((section + 1, me))

    @pl.when(is_helper)
    def _():
        pl.semaphore_wait(barrier, GROUP - 1 + 7)

    @pl.when(jnp.logical_not(has_next))
    def _():
        pl.semaphore_wait(barrier, GROUP - 1 + 5)

    @pl.when(jnp.logical_and(has_next, jnp.logical_not(is_helper)))
    def _():
        pl.semaphore_wait(barrier, GROUP - 1 + 6)

    for load in loads[:4]:
        load.wait()

    @pl.when(is_odd)
    def _():
        send(mod, next_mod, mod_sem.at[0], mod_sem.at[1], (section - 1, me))

    own_slot = jnp.where(y < 2, y, 2 + x // 2)

    def feed(patch, held, arrived):
        def spread(mates):
            for dx, dy in mates:
                send(first.at[patch], held.at[patch, block(own_slot), :],
                     token_sent.at[patch], arrived.at[patch, own_slot],
                     (section, chip(dx, dy)))

        @pl.when(y < 2)
        def _():
            spread(((2, 1), (2, 3), (0, 2)))

        @pl.when(y >= 2)
        def _():
            spread(((1, 2), (3, 2), (2, 0)))

    def to_neighbours(patch, slot, part, start, target_section, sent):
        along = ((1, 0), (3, 0)) if slot < 2 else ((0, 1), (0, 3))
        across = ((0, 1), (0, 3)) if slot < 2 else ((1, 0), (3, 0))
        for dx, dy in (across[slot % 2], *along):
            send(part, land.at[patch, pl.ds(start, rows), :], sent,
                 land_sem.at[patch, slot // 2], (target_section, chip(dx, dy)))

    def held_block(slot):
        return pl.multiple_of(held_start(x, y, slot // 2) + (slot % 2) * rows, rows)

    def exchange(patch):
        for slot in range(HELD):
            arrived = incoming.at[patch, pl.ds(slot * rows, rows), :]

            @pl.when(jnp.logical_or(jnp.logical_not(is_first), own_slot != slot))
            def _():
                wait(arrived, incoming_sem.at[patch, slot])

            start = held_block(slot)
            part = land.at[patch, pl.ds(start, rows), :]
            land[patch, pl.ds(start, rows), :] = normalized(
                arrived[...].astype(jnp.float32), mod[0], mod[1]
            )
            to_neighbours(patch, slot, part, start, section, land_sent.at[patch])

    def spot_of(place):
        spot = jnp.int32(0)
        for t in range(1, patches):
            spot = jnp.where(order[t] == place, t, spot)
        return spot

    @pl.when(is_first)
    def _():
        for patch in range(patches):
            first[patch] = tokens[order[patch]]
            incoming[patch, block(own_slot), :] = first[patch]
        feed(0, incoming, incoming_sem)

    @pl.when(is_helper)
    def _():
        for patch in range(1, patches):
            first[patch] = tokens[order[patch]]
            feed(patch, normed, early_sem)
        for patch in range(1, patches):
            for slot in range(HELD):
                @pl.when(own_slot != slot)
                def _():
                    part = normed.at[patch, slot * rows : (slot + 1) * rows, :]
                    wait(part, early_sem.at[patch, slot])
                    send(part, incoming.at[patch, slot * rows : (slot + 1) * rows, :],
                         early_sent.at[patch], incoming_sem.at[patch, slot], (0, me))
        for patch in range(1, patches):
            wait(normed.at[patch, 0 : (HELD - 1) * rows, :], early_sent.at[patch])

    @pl.when(is_even)
    def _():
        exchange(0)

    loads[4].wait()
    for patch in range(1, patches):
        place = pl.ds(patch * patch_rows, patch_rows)
        key_unit[place, :] = unit_rows(stale[0, order[patch]], gain[1:2, :]).astype(jnp.bfloat16)
        value_rows[place, :] = stale[1, order[patch]]

    for load in loads[5:8]:
        load.wait()

    def attend(patch):
        parts = []
        for kind in range(2):
            @pl.when(is_even)
            def _():
                wait(land.at[patch, pl.ds(0, 6 * rows), :], land_sem.at[patch, kind])

            @pl.when(is_odd)
            def _():
                wait(land.at[patch, pl.ds(0, 8 * rows), :], land_sem.at[patch, kind])

            parts.append(
                jnp.dot(
                    land[patch, kind * 8 * rows : (kind + 1) * 8 * rows, :], project_w[...],
                    preferred_element_type=jnp.float32,
                ).astype(jnp.bfloat16)
            )
        projected = jnp.concatenate(parts, axis=0)
        place = pl.ds(pl.multiple_of(patch * patch_rows, patch_rows), patch_rows)
        keys, values = projected[:, head : 2 * head], projected[:, 2 * head :]
        key_unit[place, :] = unit_rows(keys, gain[1:2, :]).astype(jnp.bfloat16)
        value_rows[place, :] = values
        query_unit = (
            unit_rows(projected[:, :head], gain[0:1, :]) / math.sqrt(head)
        ).astype(jnp.bfloat16)
        scores = lax.dot_general(
            query_unit, key_unit[...], (((1,), (1,)), ((), ())),
            preferred_element_type=jnp.float32,
        )
        exp_scores = jnp.exp(scores)
        denominator = jnp.sum(exp_scores, axis=-1, keepdims=True)
        summed = jnp.dot(
            exp_scores.astype(jnp.bfloat16), value_rows[...], preferred_element_type=jnp.float32
        )
        attended[...] = (summed / denominator).astype(jnp.bfloat16)

        for index, (dx, dy) in enumerate(STEPS[1:], 1):
            to_x, to_y = (x + dx) % SIDE, (y + dy) % SIDE
            for kind in range(2):
                staged[patch, index, kind * 2 * rows : (kind + 1) * 2 * rows, :] = (
                    attended[pl.ds(held_start(to_x, to_y, kind), 2 * rows), :]
                )
            seen = STEPS.index(((SIDE - dx) % SIDE, (SIDE - dy) % SIDE))
            send(staged.at[patch, index],
                 heads_land.at[patch, :, seen * head : (seen + 1) * head],
                 head_sent.at[patch], head_sem.at[patch, HOPS[index] - 1],
                 (section, to_x * SIDE + to_y))

        for kind in range(2):
            heads_land[patch, kind * 2 * rows : (kind + 1) * 2 * rows, :head] = attended[
                pl.ds(held_start(x, y, kind), 2 * rows), :
            ]
        for index, spot in enumerate(BLOCK_ORDER):
            taken = slice(index * rows, (index + 1) * rows)
            fresh[0, patch, spot * rows : (spot + 1) * rows, :] = keys[taken]
            fresh[1, patch, spot * rows : (spot + 1) * rows, :] = values[taken]

        @pl.when(patch == patches - 1)
        def _():
            for place in range(patches):
                cache_ref[0, place] = fresh[0, spot_of(place)]
                cache_ref[1, place] = fresh[1, spot_of(place)]

    def finish(patch):
        arrived = 0
        for begin, end in RUNS:
            while arrived < HOPS[end - 1]:
                arrived += 1
                wait(heads_land.at[patch, :, pl.ds(0, HOPS.count(arrived) * head)],
                     head_sem.at[patch, arrived - 1])
            weights = jnp.concatenate(
                [
                    output_w[pl.ds(pl.multiple_of(chip(dx, dy) * head, head), head), :]
                    for dx, dy in STEPS[begin:end]
                ],
                axis=0,
            )
            product = jnp.dot(
                heads_land[patch, :, begin * head : end * head], weights,
                preferred_element_type=jnp.float32,
            )
            total[...] = product if begin == 0 else total[...] + product

        @pl.when(is_odd)
        def _():
            wait(incoming.at[patch], incoming_sem.at[patch, 0])

        @pl.when(jnp.logical_and(is_even, patch == 0))
        def _():
            wait(next_mod, mod_sem.at[1])

        for slot in range(HELD):
            taken = pl.ds(slot * rows, rows)
            produced[patch, taken, :] = (
                incoming[patch, taken, :].astype(jnp.float32) + mod[2] * total[taken, :]
            ).astype(jnp.bfloat16)

            @pl.when(is_even)
            def _():
                part = normed.at[patch, taken, :]
                normed[patch, taken, :] = normalized(
                    produced[patch, taken, :].astype(jnp.float32), next_mod[0], next_mod[1]
                )
                to_neighbours(
                    patch, slot, part, held_block(slot), section + 1, normed_sent.at[patch]
                )

            @pl.when(jnp.logical_and(is_odd, has_next))
            def _():
                send(produced.at[patch, taken, :], incoming.at[patch, taken, :],
                     produced_sent.at[patch], incoming_sem.at[patch, slot], (section + 1, me))

        @pl.when(is_even)
        def _():
            for kind in range(2):
                send(normed.at[patch, pl.ds(kind * 2 * rows, 2 * rows), :],
                     land.at[patch, pl.ds(held_start(x, y, kind), 2 * rows), :],
                     normed_sent.at[patch], land_sem.at[patch, kind], (section + 1, me))
            send(produced.at[patch], incoming.at[patch],
                 produced_sent.at[patch], incoming_sem.at[patch, 0], (section + 1, me))

        results[patch] = produced[patch, block(own_slot), :]

        @pl.when(patch == patches - 1)
        def _():
            for place in range(patches):
                out_ref[place] = results[spot_of(place)]

    @pl.loop(0, patches)
    def _(patch):
        attend(patch)

        @pl.when(jnp.logical_and(is_even, patch < patches - 1))
        def _():
            exchange(patch + 1)

        @pl.when(patch == 0)
        def _():
            loads[8].wait()

        finish(patch)

    @pl.when(is_odd)
    def _():
        wait(next_mod, mod_sem.at[0])

    @pl.loop(0, patches)
    def _(patch):
        wait(heads_land.at[patch, :, pl.ds(0, (GROUP - 1) * head)], head_sent.at[patch])

        @pl.when(is_even)
        def _():
            wait(land.at[patch, pl.ds(0, 3 * HELD * rows), :], land_sent.at[patch])
            wait(land.at[patch], normed_sent.at[patch])

        @pl.when(
            jnp.logical_or(
                jnp.logical_and(is_first, patch == 0), jnp.logical_and(is_helper, patch > 0)
            )
        )
        def _():
            wait(incoming.at[patch, pl.ds(0, 3 * rows), :], token_sent.at[patch])

        @pl.when(has_next)
        def _():
            wait(produced.at[patch], produced_sent.at[patch])


def copy_kernel(out_ref, cache_ref, out_to, cache_to, out_held, cache_held, sem):
    pieces = [
        (held.at[part], source.at[part], target.at[part], index, part)
        for index, (held, source, target) in enumerate(
            ((cache_held, cache_ref, cache_to), (out_held, out_ref, out_to))
        )
        for part in range(source.shape[0])
    ]
    inward = [
        pltpu.make_async_copy(source, held, sem.at[0, index, part])
        for held, source, _, index, part in pieces
    ]
    outward = [
        pltpu.make_async_copy(held, target, sem.at[1, index, part])
        for held, _, target, index, part in pieces
    ]
    for copy in inward:
        copy.start()
    for copy, onward in zip(inward, outward):
        copy.wait()
        onward.start()
    for copy in outward:
        copy.wait()


def body(
    patch_tokens, patch_order, modulation, norm_gain, project_weight, output_weight, stale_cache
):
    sections = lax.axis_size("section")
    patches, rows, width = patch_tokens.shape
    head = project_weight.shape[-1]
    patch_rows = rows * GROUP
    tokens = patches * patch_rows
    columns = project_weight.reshape(width, 3, head).transpose(1, 0, 2)
    vmem, hbm = pl.BlockSpec(memory_space=pltpu.VMEM), pl.BlockSpec(memory_space=pltpu.HBM)
    bf16, f32, dma = jnp.bfloat16, jnp.float32, pltpu.SemaphoreType.DMA
    shapes = (
        jax.ShapeDtypeStruct((patches, rows, width), jnp.bfloat16),
        jax.ShapeDtypeStruct((2, patches, patch_rows, head), jnp.bfloat16),
    )
    results, cache = pl.pallas_call(
        functools.partial(kernel, sections, patches, rows, width, head),
        out_shape=shapes,
        in_specs=[hbm] * 7,
        out_specs=(vmem, vmem),
        scratch_shapes=[
            pltpu.SMEM((patches,), jnp.int32),
            pltpu.VMEM((patches, rows, width), bf16),
            pltpu.VMEM((3, 1, width), f32),
            pltpu.VMEM((2, head), f32),
            pltpu.VMEM((2, patches, patch_rows, head), bf16),
            pltpu.VMEM((width, 3 * head), bf16),
            pltpu.VMEM((GROUP * head, width), bf16),
            pltpu.VMEM((patches, rows, width), bf16),
            pltpu.VMEM((patches, HELD * rows, width), bf16),
            pltpu.VMEM((patches, HELD * rows, width), bf16),
            pltpu.VMEM((patches, patch_rows, width), bf16),
            pltpu.VMEM((patch_rows, head), bf16),
            pltpu.VMEM((patches, GROUP, HELD * rows, head), bf16),
            pltpu.VMEM((patches, HELD * rows, GROUP * head), bf16),
            pltpu.VMEM((tokens, head), bf16),
            pltpu.VMEM((tokens, head), bf16),
            pltpu.VMEM((HELD * rows, width), f32),
            pltpu.VMEM((patches, rows, width), bf16),
            pltpu.VMEM((2, patches, patch_rows, head), bf16),
            pltpu.VMEM((3, 1, width), f32),
            pltpu.VMEM((patches, HELD * rows, width), bf16),
            dma((2,)), dma((patches,)), dma((patches, HELD)), dma((patches,)),
            dma((9,)), dma((patches,)), dma((patches, HELD)), dma((patches,)), dma((patches, 2)),
            dma((patches,)), dma((patches, SIDE)), dma((patches,)),
        ],
        compiler_params=pltpu.CompilerParams(
            collective_id=0, has_side_effects=True, vmem_limit_bytes=58 << 20
        ),
        name="blocks",
    )(
        patch_tokens, patch_order, modulation.reshape(3, 1, width), norm_gain[0], columns,
        output_weight[0], stale_cache.reshape(2, patches, patch_rows, head),
    )
    results, cache = pl.pallas_call(
        copy_kernel,
        out_shape=shapes,
        in_specs=[hbm] * 2,
        out_specs=(hbm, hbm),
        scratch_shapes=[
            pltpu.VMEM((patches, rows, width), bf16),
            pltpu.VMEM((2, patches, patch_rows, head), bf16),
            dma((2, 2, patches)),
        ],
        name="results",
    )(results, cache)
    return (results[None], cache.reshape(1, 2, patches, patch_rows, 1, head))


def solution(mesh):
    in_specs = (
        P(None, "seq", None),
        P(),
        P("section", None, None),
        P("section", None, None),
        P("section", None, None, "seq", None),
        P("section", None, None),
        P("section", None, None, None, "seq", None),
    )
    out_specs = (P("section", None, "seq", None), P("section", None, None, None, "seq", None))
    return jax.shard_map(body, mesh=mesh, in_specs=in_specs, out_specs=out_specs, check_vma=False)
```
